32 devices in a mesh: fsdp: 16 (over z, y, core), ctx: 2 (over x).
Axes of the slice: x: 2, y: 2, z: 4, core: 2. Of those that a mesh axis runs over, the one named last changes fastest.
Arguments:
- queries: bfloat16 [16, 256, 1536], P('fsdp', 'ctx'), may hold values from -1.6953125 to 1.6953125
- key_states: bfloat16 [16, 256, 1536], P('fsdp', 'ctx'), may hold values from -1.6953125 to 1.6953125
- value_states: bfloat16 [16, 256, 1536], P('fsdp', 'ctx'), may hold values from -6 to 6
- attn_out: bfloat16 [16, 256, 1536], P('fsdp', 'ctx'), may hold values from -6 to 6
- log_norm: bfloat16 [16, 256, 12], P('fsdp', 'ctx'), may hold values from 3 to 4.5
- out_grad: bfloat16 [16, 256, 3072], P('fsdp', 'ctx'), may hold values from -6 to 6
- proj_weight: bfloat16 [1536, 3072], P('fsdp', 'ctx'), may hold values from -0.109375 to 0.109375
- tile_mask: int32 [16, 12, 4, 4], P('fsdp'), may hold values from 0 to 1, as said below
Outputs:
- grad_query: bfloat16 [16, 256, 1536], P('fsdp', 'ctx')
- grad_key: bfloat16 [16, 256, 1536], P('fsdp', 'ctx')
- grad_value: bfloat16 [16, 256, 1536], P('fsdp', 'ctx')
The draws below stay inside these ranges and needn't reach their ends.
Inputs may be any that keep to these rules, and one draw needn't show every extreme that they name: tile_mask[c, h, i, j] = 1 lets the query tokens of tile i attend to the key tokens of tile j in head h; a tile is 64 consecutive tokens; every tile attends to itself.
All inputs are finite; a program needn't handle non-finite values.
Results may differ from the reference program's by a relative error of at most 0.014.
Values may be sent and summed in bfloat16 or wider, within the bound.
A program may use at most 64 MiB of HBM per device.

```python
import jax
import jax.numpy as jnp
from jax import lax

D = 3072
H = 12
HD = 128
TILE = 64
TOK_DEV = 128
CLIPS = 16
SEQ = 256
HID = 1536
NT = 4
N_CTX = 2


def draw_tile_mask(key, part):
    rate_key, roll_key = jax.random.split(key, 2)
    rates = jax.random.randint(rate_key, (CLIPS, 1, NT, 1), 30, 900)
    rolls = jax.random.randint(roll_key, (CLIPS, H, NT, NT), 0, 1000)
    diagonal_term = jnp.arange(NT)[:, None] == jnp.arange(NT)[None, :]
    return jnp.where((rolls < rates) | diagonal_term[None, None], 1, 0).astype(jnp.int32)


def steps_of(key, shape, cuts, least, largest):
    level = 1.0
    for dim, shards_of in cuts:
        draws = jax.random.uniform(jax.random.fold_in(jax.random.fold_in(key, 6), dim), (shards_of,), jnp.float32, least / len(cuts), largest / len(cuts))
        level = level * jnp.repeat(jnp.exp(draws), shape[dim] // shards_of).reshape((-1,) + (1,) * (len(shape) - 1 - dim))
    return level


def normal_values(key, extent, deviation, most, cuts=(), held_as=jnp.bfloat16):
    gain = steps_of(key, extent, cuts, -0.22, 0.18) if cuts else 1.0
    values = jax.random.normal(key, extent, jnp.float32) * deviation * gain
    return jnp.minimum(jnp.maximum(values, -most), most).astype(held_as)


def setup_inputs(seed: int = 0) -> dict:
    arg_keys = jax.random.split(jax.random.key(seed), 9)
    queries = jnp.clip(jax.random.uniform(arg_keys[0], (CLIPS, SEQ, HID), jnp.float32, -1.6953125, 1.6953125) * steps_of(arg_keys[0], (CLIPS, SEQ, HID), ((0, 16), (1, 2)), -0.4, 0.0), -1.6953125, 1.6953125).astype(jnp.bfloat16)
    key_states = jnp.clip(jax.random.uniform(arg_keys[1], (CLIPS, SEQ, HID), jnp.float32, -1.6953125, 1.6953125) * steps_of(arg_keys[1], (CLIPS, SEQ, HID), ((0, 16), (1, 2)), -0.4, 0.0), -1.6953125, 1.6953125).astype(jnp.bfloat16)
    value_states = normal_values(arg_keys[2], (CLIPS, SEQ, HID), 1.0, 6.0, ((0, 16), (1, 2)))
    attn_out = normal_values(arg_keys[3], (CLIPS, SEQ, HID), 1.0, 6.0, ((0, 16), (1, 2)))
    log_norm = jnp.clip(3.0 + 1.5 * jax.random.uniform(arg_keys[4], (CLIPS, SEQ, H), jnp.float32) ** steps_of(arg_keys[4], (CLIPS, SEQ, H), ((0, 16), (1, 2)), -0.2, 0.2), 3.0, 4.5).astype(jnp.bfloat16)
    out_grad = normal_values(arg_keys[5], (CLIPS, SEQ, D), 1.0, 6.0, ((0, 16), (1, 2)))
    proj_weight = normal_values(arg_keys[6], (HID, D), D ** -0.5, 0.109375, ((0, 16), (1, 2)))
    tile_mask = draw_tile_mask(jax.random.fold_in(arg_keys[8], 71), 0)
    return {"queries": queries, "key_states": key_states, "value_states": value_states, "attn_out": attn_out, "log_norm": log_norm, "out_grad": out_grad, "proj_weight": proj_weight, "tile_mask": tile_mask}


def round_trip(array):
    return lax.optimization_barrier(array.astype(jnp.bfloat16)).astype(jnp.float32)


def reference(queries, key_states, value_states, attn_out, log_norm, out_grad, proj_weight, tile_mask):
    score_scale = HD ** -0.5
    slab_width = D // N_CTX
    weight_blocks = proj_weight.astype(jnp.float32).reshape(H * HD, N_CTX, slab_width)
    tile_ids = jnp.arange(SEQ, dtype=jnp.int32) // TILE

    def one_clip(inputs):
        query_row_block, key_rows, value_rows, out_rows, norm_rows, grad_rows, table = inputs
        grad_blocks = grad_rows.astype(jnp.float32).reshape(SEQ, N_CTX, slab_width)
        weight_part = jnp.einsum('lbw,hbw->blh', grad_blocks, weight_blocks)
        attn_grad = jnp.sum(round_trip(weight_part), axis=0).astype(jnp.bfloat16)
        gradient_by_head = attn_grad.astype(jnp.float32).reshape(SEQ, H, HD)
        out_heads = out_rows.astype(jnp.float32).reshape(SEQ, H, HD)
        row_dots = round_trip(jnp.sum(gradient_by_head * out_heads, axis=-1))
        allowed = table[:, tile_ids[:, None], tile_ids[None, :]].astype(jnp.float32)
        query_head_rows = query_row_block.astype(jnp.float32).reshape(SEQ, H, HD)
        key_head_rows = key_rows.astype(jnp.float32).reshape(SEQ, H, HD)
        value_head_rows = value_rows.astype(jnp.float32).reshape(SEQ, H, HD)
        scores = jnp.einsum('thd,shd->hts', query_head_rows, key_head_rows) * score_scale
        attn_prob = jnp.exp(scores - norm_rows.astype(jnp.float32).T[:, :, None]) * allowed
        prob_grad = jnp.einsum('thd,shd->hts', gradient_by_head, value_head_rows)
        score_grad = attn_prob * (prob_grad - row_dots.T[:, :, None])
        probability_per_round = round_trip(attn_prob)
        gradient_per_round = round_trip(score_grad)
        by_query = probability_per_round.reshape(H, N_CTX, TOK_DEV, SEQ)
        grad_by_query = gradient_per_round.reshape(H, N_CTX, TOK_DEV, SEQ)
        value_part = jnp.einsum('hbts,bthd->bshd', by_query, gradient_by_head.reshape(N_CTX, TOK_DEV, H, HD))
        key_part = score_scale * jnp.einsum('hbts,bthd->bshd', grad_by_query, query_head_rows.reshape(N_CTX, TOK_DEV, H, HD))
        query_part = score_scale * jnp.einsum('htbs,bshd->bthd', gradient_per_round.reshape(H, SEQ, N_CTX, TOK_DEV), key_head_rows.reshape(N_CTX, TOK_DEV, H, HD))
        grad_value = jnp.sum(round_trip(value_part), axis=0).astype(jnp.bfloat16).reshape(SEQ, H * HD)
        grad_key = jnp.sum(round_trip(key_part), axis=0).astype(jnp.bfloat16).reshape(SEQ, H * HD)
        grad_query = jnp.sum(round_trip(query_part), axis=0).astype(jnp.bfloat16).reshape(SEQ, H * HD)
        return grad_query, grad_key, grad_value

    grad_query, grad_key, grad_value = lax.map(one_clip, (queries, key_states, value_states, attn_out, log_norm, out_grad, tile_mask))
    return (grad_query, grad_key, grad_value)
```

```python
import functools

import jax
import jax.numpy as jnp
from jax import lax
from jax.experimental import pallas as pl
from jax.experimental.pallas import tpu as pltpu
from jax.sharding import PartitionSpec as P

H = 12
HD = 128
TILE = 64


def round_trip(array):
    return lax.optimization_barrier(array.astype(jnp.bfloat16)).astype(jnp.float32)


def tile_onehot(row_count, tile_count):
    tile_ids = jnp.arange(row_count, dtype=jnp.int32) // TILE
    return (tile_ids[:, None] == jnp.arange(tile_count, dtype=jnp.int32)[None, :]).astype(
        jnp.float32
    )


def score_terms(
    query_head_rows, gradient_by_head, norm_rows, dots_rows, key_head_rows, value_head_rows, allowed
):
    score_scale = HD ** (-0.5)
    scores = (
        jnp.einsum(
            "vgl,ygl->gvy", query_head_rows, key_head_rows, preferred_element_type=jnp.float32
        )
        * score_scale
    )
    attn_prob = jnp.exp(scores - norm_rows.T[:, :, None]) * allowed
    prob_grad = jnp.einsum(
        "vgl,ygl->gvy", gradient_by_head, value_head_rows, preferred_element_type=jnp.float32
    )
    score_grad = attn_prob * (prob_grad - dots_rows.T[:, :, None])
    return (attn_prob.astype(jnp.bfloat16), score_grad.astype(jnp.bfloat16))


def local(queries, key_states, value_states, attn_out, log_norm, out_grad, proj_weight, tile_mask):
    ctx_count = lax.axis_size("ctx")
    ctx_index = lax.axis_index("ctx")
    tok_rows = queries.shape[1]
    hid_width = queries.shape[2]
    score_scale = HD ** (-0.5)
    tile_table = tile_mask[0]
    tile_count = tile_table.shape[1]
    own_count = tok_rows // TILE
    grad_slab = lax.all_to_all(out_grad[0], "ctx", split_axis=1, concat_axis=0, tiled=True)
    product = lax.dot_general(
        grad_slab,
        lax.all_gather(proj_weight, "fsdp", axis=0, tiled=True),
        (((1,), (1,)), ((), ())),
        preferred_element_type=jnp.float32,
    )
    partial_value = product.astype(jnp.bfloat16)
    arrived = lax.all_to_all(
        partial_value.reshape(ctx_count, tok_rows, hid_width),
        "ctx",
        split_axis=0,
        concat_axis=0,
        tiled=True,
    )
    attn_grad = jnp.sum(arrived.astype(jnp.float32), axis=0).astype(jnp.bfloat16)
    query_head_rows = queries[0].reshape(tok_rows, H, HD)
    gradient_by_head = attn_grad.reshape(tok_rows, H, HD)
    out_heads = attn_out[0].reshape(tok_rows, H, HD)
    dots_round = jnp.sum(
        gradient_by_head.astype(jnp.float32) * out_heads.astype(jnp.float32), axis=-1
    ).astype(jnp.bfloat16)
    own_rows = jnp.repeat(
        lax.dynamic_slice_in_dim(tile_table, ctx_index * own_count, own_count, 1).astype(
            jnp.float32
        ),
        TILE,
        axis=1,
    )
    norm_rows = log_norm[0].astype(jnp.float32)
    dots_rows = lax.optimization_barrier(dots_round).astype(jnp.float32)
    key_rows = lax.all_gather(key_states[0], "ctx", axis=0, tiled=True)
    value_rows = lax.all_gather(value_states[0], "ctx", axis=0, tiled=True)
    piece_rows = key_rows.shape[0]
    sub_rows = min(piece_rows, tok_rows)
    blocks_in = piece_rows // sub_rows
    key_block = key_rows.reshape(piece_rows, H, HD)
    value_block = value_rows.reshape(piece_rows, H, HD)
    allowed = jnp.einsum("htn,mn->htm", own_rows, tile_onehot(piece_rows, tile_count))
    probability_per_round, gradient_per_round = score_terms(
        query_head_rows, gradient_by_head, norm_rows, dots_rows, key_block, value_block, allowed
    )
    value_term = jnp.einsum(
        "bve,vbt->ebt", probability_per_round, gradient_by_head, preferred_element_type=jnp.float32
    )
    key_term = (
        jnp.einsum(
            "bve,vbt->ebt", gradient_per_round, query_head_rows, preferred_element_type=jnp.float32
        )
        * score_scale
    )
    query_term = (
        jnp.einsum(
            "hmbn,bnhd->bmhd",
            gradient_per_round.reshape(H, tok_rows, blocks_in, sub_rows),
            key_block.reshape(blocks_in, sub_rows, H, HD),
            preferred_element_type=jnp.float32,
        )
        * score_scale
    )
    part_slots = query_term.reshape(blocks_in, tok_rows, hid_width)
    key_total = key_term.reshape(piece_rows, hid_width)
    value_total = value_term.reshape(piece_rows, hid_width)
    part_slots, key_total, value_total = (part_slots, key_total, value_total)
    grad_query = jnp.sum(round_trip(part_slots), axis=0).astype(jnp.bfloat16)
    key_parts, value_parts = (
        lax.all_to_all(
            key_total.astype(jnp.bfloat16).reshape(ctx_count, tok_rows, hid_width),
            "ctx",
            split_axis=0,
            concat_axis=0,
            tiled=True,
        ),
        lax.all_to_all(
            value_total.astype(jnp.bfloat16).reshape(ctx_count, tok_rows, hid_width),
            "ctx",
            split_axis=0,
            concat_axis=0,
            tiled=True,
        ),
    )
    grad_key = jnp.sum(key_parts.astype(jnp.float32), axis=0).astype(jnp.bfloat16)
    grad_value = jnp.sum(value_parts.astype(jnp.float32), axis=0).astype(jnp.bfloat16)
    return (grad_query[None], grad_key[None], grad_value[None])


MESH = pl.DeviceIdType.MESH
CHUNKS = 2
UP, DOWN, ACROSS, SIBLING = range(4)


def dot(a, b, a_dim, b_dim):
    return lax.dot_general(
        a, b, (((a_dim,), (b_dim,)), ((), ())), preferred_element_type=jnp.float32
    )


def fused_kernel(
    q_ref, k_ref, v_ref, o_ref, ln_ref, og_ref, w_ref, mask_ref,
    gq_ref, gk_ref, gv_ref,
    wbuf, og_all, q_all, ln_all, p_all, part_own, part_in, grad, dots, dq_out, dq_in,
    w_send, w_recv, x_send, x_recv,
):
    layers = wbuf.shape[0]
    chunk_rows = wbuf.shape[4]
    tok = q_ref.shape[1]
    heads = ln_ref.shape[2]
    width = w_ref.shape[1]
    group_width = grad.shape[2]
    per_group = heads // layers
    hd = group_width // per_group
    tile = 2 * tok // mask_ref.shape[3]
    own_tiles = tok // tile
    scale = hd ** (-0.5)

    f = lax.axis_index("fsdp")
    x = lax.axis_index("ctx")
    core = lax.rem(f, 2)
    y = lax.rem(lax.div(f, 2), 2)
    z = lax.div(f, 4)
    other = 1 - x

    def place(zz, yy, cc):
        return ((zz * 2 + yy) * 2 + cc, x)

    partner = (f, other)
    targets = {
        UP: place(z + 1, y, core),
        DOWN: place(z - 1, y, core),
        ACROSS: place(z, 1 - y, core),
        SIBLING: place(z, y, 1 - core),
    }
    has_up = z < layers - 1
    has_down = z > 0

    barrier = pltpu.get_barrier_semaphore()
    for device in (partner, targets[ACROSS], targets[SIBLING]):
        pl.semaphore_signal(barrier, inc=1, device_id=device, device_id_type=MESH)

    @pl.when(has_up)
    def _():
        pl.semaphore_signal(barrier, inc=1, device_id=targets[UP], device_id_type=MESH)

    @pl.when(has_down)
    def _():
        pl.semaphore_signal(barrier, inc=1, device_id=targets[DOWN], device_id_type=MESH)

    pl.semaphore_wait(barrier, 3 + has_up.astype(jnp.int32) + has_down.astype(jnp.int32))

    def weight_copy(zz, yy, cc, ch, way, own=False):
        slot = wbuf.at[zz, yy, cc, ch]
        source = w_ref.at[pl.ds(ch * chunk_rows, chunk_rows)] if own else slot
        return pltpu.make_async_remote_copy(
            src_ref=source,
            dst_ref=slot,
            send_sem=w_send.at[zz, yy, cc, ch, way],
            recv_sem=w_recv.at[zz, yy, cc, ch],
            device_id=targets[way],
            device_id_type=MESH,
        )

    def x_copy(source, target, kind, k=0):
        return pltpu.make_async_remote_copy(
            src_ref=source,
            dst_ref=target,
            send_sem=x_send.at[kind, k],
            recv_sem=x_recv.at[kind, k],
            device_id=partner,
            device_id_type=MESH,
        )

    og_copy = x_copy(
        og_ref.at[0, :, pl.ds(pl.multiple_of(other * width, width), width)],
        og_all.at[pl.ds(tok, tok)],
        0,
    )
    q_copy = x_copy(q_ref.at[0], q_all.at[pl.ds(tok, tok)], 1)
    ln_copy = x_copy(ln_all.at[0], ln_all.at[1], 2)

    def part_copies(k):
        return (
            x_copy(part_own.at[k, pl.ds(tok, tok)], part_in.at[k, pl.ds(0, tok)], 3, k),
            x_copy(part_own.at[k, pl.ds(0, tok)], part_in.at[k, pl.ds(tok, tok)], 4, k),
        )

    def dots_copy(k):
        return x_copy(dots.at[k, 0], dots.at[k, 1], 5, k)

    def dq_copy(k):
        return x_copy(dq_out.at[k], dq_in.at[k], 6, k)

    def own_weight(action):
        for ch in range(CHUNKS):
            for way, there in ((UP, has_up), (DOWN, has_down), (ACROSS, None), (SIBLING, None)):
                def run(way=way, ch=ch):
                    action(weight_copy(z, y, core, ch, way, True))

                if there is None:
                    run()
                else:
                    pl.when(there)(run)

    own_weight(lambda copy: copy.start())
    og_copy.start()
    ln_all[0] = jnp.zeros(ln_all.shape[1:], ln_all.dtype)
    ln_all[0, :, pl.ds(0, heads)] = ln_ref[0]
    ln_copy.start()

    def handle_z(d):
        for ch in range(CHUNKS):

            @pl.when(z >= d)
            def _(ch=ch):
                weight_copy(z - d, y, core, ch, SIBLING).wait_recv()

                @pl.when(has_up)
                def _():
                    weight_copy(z - d, y, core, ch, UP).start()

                weight_copy(z - d, y, core, ch, ACROSS).start()
                weight_copy(z - d, y, core, ch, SIBLING).start()

            @pl.when(z + d < layers)
            def _(ch=ch):
                weight_copy(z + d, y, core, ch, SIBLING).wait_recv()

                @pl.when(has_down)
                def _():
                    weight_copy(z + d, y, core, ch, DOWN).start()

                weight_copy(z + d, y, core, ch, ACROSS).start()
                weight_copy(z + d, y, core, ch, SIBLING).start()

    def handle_y(d):
        for ch in range(CHUNKS):

            @pl.when(z >= d)
            def _(ch=ch):
                weight_copy(z - d, 1 - y, core, ch, SIBLING).wait_recv()
                weight_copy(z - d, 1 - y, core, ch, SIBLING).start()

            if d:

                @pl.when(z + d < layers)
                def _(ch=ch):
                    weight_copy(z + d, 1 - y, core, ch, SIBLING).wait_recv()
                    weight_copy(z + d, 1 - y, core, ch, SIBLING).start()

    def wait_siblings(g):
        for ch in range(CHUNKS):
            weight_copy(g, y, 1 - core, ch, SIBLING).wait_recv()
            weight_copy(g, 1 - y, 1 - core, ch, SIBLING).wait_recv()

    turn = 1 - 2 * lax.div(z, layers // 2)

    def layer(k):
        return lax.rem(z + turn * k + layers, layers)

    lane_tile = lax.div(lax.broadcasted_iota(jnp.int32, (1, tok), 1), tile)

    def probabilities(b, owner):
        norm = ln_all[b].astype(jnp.float32)
        for h in range(heads):
            cols = pl.ds(h * hd, hd)
            scores = dot(q_all[pl.ds(b * tok, tok), cols], k_ref[0, :, cols], 1, 1) * scale
            prob = jnp.exp(scores - norm[:, h : h + 1])
            for i in range(own_tiles):
                allowed = jnp.zeros((1, tok), jnp.float32)
                for j in range(own_tiles):
                    flag = mask_ref[0, h, owner * own_tiles + i, x * own_tiles + j]
                    allowed = jnp.where(lane_tile == j, flag.astype(jnp.float32), allowed)
                p_all[h, pl.ds(b * tok + i * tile, tile), :] = (
                    prob[i * tile : (i + 1) * tile] * allowed
                )

    def project(k):
        g = layer(k)
        wait_siblings(g)
        w = wbuf[g].reshape(group_width, width)
        for b in (1, 0):
            part = dot(og_all[pl.ds(b * tok, tok)], w, 1, 1)
            part_own[k, pl.ds(b * tok, tok)] = part.astype(jnp.bfloat16)
            part_copies(k)[1 - b].start()

    lane = lax.broadcasted_iota(jnp.int32, (tok, dots.shape[3]), 1)

    def reduce(k):
        g = layer(k)
        for copy in part_copies(k):
            copy.wait_recv()
        total = part_own[k].astype(jnp.float32) + part_in[k].astype(jnp.float32)
        total = total.astype(jnp.bfloat16)
        grad[k] = total
        own = total[:tok].astype(jnp.float32)
        row = jnp.zeros(lane.shape, jnp.float32)
        for j in range(per_group):
            cols = pl.ds(pl.multiple_of((g * per_group + j) * hd, hd), hd)
            prod = own[:, j * hd : (j + 1) * hd] * o_ref[0, :, cols].astype(jnp.float32)
            row = jnp.where(lane == j, jnp.sum(prod, axis=1, keepdims=True), row)
        dots[k, 0] = row.astype(jnp.bfloat16)
        dots_copy(k).start()

    def attend(k):
        g = layer(k)
        dots_copy(k).wait_recv()
        row = dots[k].reshape(2 * tok, dots.shape[3]).astype(jnp.float32)
        for j in range(per_group):
            h = g * per_group + j
            cols = pl.ds(pl.multiple_of(h * hd, hd), hd)
            prob = p_all[h]
            grad_rows = grad[k, :, pl.ds(j * hd, hd)]
            prob_grad = dot(grad_rows, v_ref[0, :, cols], 1, 1)
            score_grad = (prob * (prob_grad - row[:, j : j + 1])).astype(jnp.bfloat16)
            part = dot(score_grad, k_ref[0, :, cols], 1, 0) * scale
            part = part.astype(jnp.bfloat16)
            dq_out[k, :, pl.ds(j * hd, hd)] = part[tok:]
            gq_ref[0, :, cols] = part[:tok]
            gv_ref[0, :, cols] = dot(prob.astype(jnp.bfloat16), grad_rows, 0, 0).astype(
                jnp.bfloat16
            )
            gk_ref[0, :, cols] = (dot(score_grad, q_all[:, cols], 0, 0) * scale).astype(
                jnp.bfloat16
            )
        dq_copy(k).start()

    def finish(k):
        g = layer(k)
        cols = pl.ds(pl.multiple_of(g * group_width, group_width), group_width)
        dq_copy(k).wait_recv()
        gq_ref[0, :, cols] = (
            gq_ref[0, :, cols].astype(jnp.float32) + dq_in[k].astype(jnp.float32)
        ).astype(jnp.bfloat16)

    for ch in range(CHUNKS):
        wbuf[z, y, core, ch] = w_ref[pl.ds(ch * chunk_rows, chunk_rows), :]
    og_all[pl.ds(0, tok)] = og_ref[0, :, pl.ds(pl.multiple_of(x * width, width), width)]
    q_all[pl.ds(0, tok)] = q_ref[0]
    handle_y(0)
    probabilities(0, x)
    og_copy.wait_recv()
    q_copy.start()
    for k in range(layers + 3):
        if k < layers:
            if k > 0:
                handle_y(k)
            project(k)
            if k + 1 < layers:
                handle_z(k + 1)
        if k == 1:
            ln_copy.wait_recv()
            q_copy.wait_recv()
            probabilities(1, other)
        if 0 <= k - 1 < layers:
            reduce(k - 1)
        if 0 <= k - 2 < layers:
            attend(k - 2)
        if 0 <= k - 3 < layers:
            finish(k - 3)

    own_weight(lambda copy: copy.wait_send())
    for ch in range(CHUNKS):
        weight_copy(z, 1 - y, core, ch, SIBLING).wait_send()
    for d in range(1, layers):
        for ch in range(CHUNKS):

            @pl.when(z >= d)
            def _(ch=ch, d=d):
                @pl.when(has_up)
                def _():
                    weight_copy(z - d, y, core, ch, UP).wait_send()

                weight_copy(z - d, y, core, ch, ACROSS).wait_send()
                weight_copy(z - d, y, core, ch, SIBLING).wait_send()
                weight_copy(z - d, 1 - y, core, ch, SIBLING).wait_send()

            @pl.when(z + d < layers)
            def _(ch=ch, d=d):
                @pl.when(has_down)
                def _():
                    weight_copy(z + d, y, core, ch, DOWN).wait_send()

                weight_copy(z + d, y, core, ch, ACROSS).wait_send()
                weight_copy(z + d, y, core, ch, SIBLING).wait_send()
                weight_copy(z + d, 1 - y, core, ch, SIBLING).wait_send()

    og_copy.wait_send()
    q_copy.wait_send()
    ln_copy.wait_send()
    for k in range(layers):
        for copy in part_copies(k):
            copy.wait_send()
        dots_copy(k).wait_send()
        dq_copy(k).wait_send()


def fits_kernel(queries, key_states, value_states, attn_out, log_norm, out_grad, proj_weight, tile_mask):
    fsdp = lax.axis_size("fsdp")
    heads = log_norm.shape[2]
    tok = queries.shape[1]
    rows = proj_weight.shape[0]
    if lax.axis_size("ctx") != 2 or fsdp % 8 or queries.shape[0] != 1:
        return False
    layers = fsdp // 4
    head_size = queries.shape[2] // heads
    return (
        heads % layers == 0
        and rows % (16 * CHUNKS) == 0
        and head_size == 128
        and tok % 128 == 0
        and tok % (2 * tok // tile_mask.shape[3]) == 0
        and proj_weight.shape[1] % 128 == 0
    )


def fused(queries, key_states, value_states, attn_out, log_norm, out_grad, proj_weight, tile_mask):
    layers = lax.axis_size("fsdp") // 4
    tok, hid = queries.shape[1:]
    rows, width = proj_weight.shape
    heads = log_norm.shape[2]
    group = hid // layers
    bf16 = jnp.bfloat16
    whole = pl.BlockSpec(memory_space=pltpu.VMEM)
    return tuple(pl.pallas_call(
        fused_kernel,
        out_shape=[jax.ShapeDtypeStruct(queries.shape, bf16)] * 3,
        in_specs=[whole] * 7 + [pl.BlockSpec(memory_space=pltpu.SMEM)],
        out_specs=[whole] * 3,
        scratch_shapes=[
            pltpu.VMEM((layers, 2, 2, CHUNKS, rows // CHUNKS, width), bf16),
            pltpu.VMEM((2 * tok, width), bf16),
            pltpu.VMEM((2 * tok, hid), bf16),
            pltpu.VMEM((2, tok, 128), bf16),
            pltpu.VMEM((heads, 2 * tok, tok), jnp.float32),
            pltpu.VMEM((layers, 2 * tok, group), bf16),
            pltpu.VMEM((layers, 2 * tok, group), bf16),
            pltpu.VMEM((layers, 2 * tok, group), bf16),
            pltpu.VMEM((layers, 2, tok, 128), bf16),
            pltpu.VMEM((layers, tok, group), bf16),
            pltpu.VMEM((layers, tok, group), bf16),
            pltpu.SemaphoreType.DMA((layers, 2, 2, CHUNKS, 4)),
            pltpu.SemaphoreType.DMA((layers, 2, 2, CHUNKS)),
            pltpu.SemaphoreType.DMA((7, layers)),
            pltpu.SemaphoreType.DMA((7, layers)),
        ],
        compiler_params=pltpu.CompilerParams(
            collective_id=0, has_side_effects=True, vmem_limit_bytes=40 * 1024 * 1024
        ),
    )(queries, key_states, value_states, attn_out, log_norm, out_grad, proj_weight, tile_mask))


def plan(*arrays):
    if fits_kernel(*arrays):
        return fused(*arrays)
    return local(*arrays)


def solution(mesh):
    placed = (
        P("fsdp", "ctx", None),
        P("fsdp", "ctx", None),
        P("fsdp", "ctx", None),
        P("fsdp", "ctx", None),
        P("fsdp", "ctx", None),
        P("fsdp", "ctx", None),
        P("fsdp", "ctx"),
        P("fsdp", None, None, None),
    )
    return jax.shard_map(
        plan,
        mesh=mesh,
        in_specs=placed,
        out_specs=(P("fsdp", "ctx", None), P("fsdp", "ctx", None), P("fsdp", "ctx", None)),
        check_vma=False,
    )
```

```python
import functools

import jax
import jax.numpy as jnp
from jax import lax
from jax.experimental import pallas as pl
from jax.experimental.pallas import tpu as pltpu
from jax.sharding import PartitionSpec as P

H = 12
HD = 128
TILE = 64


def round_trip(array):
    return lax.optimization_barrier(array.astype(jnp.bfloat16)).astype(jnp.float32)


def tile_onehot(row_count, tile_count):
    tile_ids = jnp.arange(row_count, dtype=jnp.int32) // TILE
    return (tile_ids[:, None] == jnp.arange(tile_count, dtype=jnp.int32)[None, :]).astype(
        jnp.float32
    )


def score_terms(
    query_head_rows, gradient_by_head, norm_rows, dots_rows, key_head_rows, value_head_rows, allowed
):
    score_scale = HD ** (-0.5)
    scores = (
        jnp.einsum(
            "vgl,ygl->gvy", query_head_rows, key_head_rows, preferred_element_type=jnp.float32
        )
        * score_scale
    )
    attn_prob = jnp.exp(scores - norm_rows.T[:, :, None]) * allowed
    prob_grad = jnp.einsum(
        "vgl,ygl->gvy", gradient_by_head, value_head_rows, preferred_element_type=jnp.float32
    )
    score_grad = attn_prob * (prob_grad - dots_rows.T[:, :, None])
    return (attn_prob.astype(jnp.bfloat16), score_grad.astype(jnp.bfloat16))


def local(queries, key_states, value_states, attn_out, log_norm, out_grad, proj_weight, tile_mask):
    ctx_count = lax.axis_size("ctx")
    ctx_index = lax.axis_index("ctx")
    tok_rows = queries.shape[1]
    hid_width = queries.shape[2]
    score_scale = HD ** (-0.5)
    tile_table = tile_mask[0]
    tile_count = tile_table.shape[1]
    own_count = tok_rows // TILE
    grad_slab = lax.all_to_all(out_grad[0], "ctx", split_axis=1, concat_axis=0, tiled=True)
    product = lax.dot_general(
        grad_slab,
        lax.all_gather(proj_weight, "fsdp", axis=0, tiled=True),
        (((1,), (1,)), ((), ())),
        preferred_element_type=jnp.float32,
    )
    partial_value = product.astype(jnp.bfloat16)
    arrived = lax.all_to_all(
        partial_value.reshape(ctx_count, tok_rows, hid_width),
        "ctx",
        split_axis=0,
        concat_axis=0,
        tiled=True,
    )
    attn_grad = jnp.sum(arrived.astype(jnp.float32), axis=0).astype(jnp.bfloat16)
    query_head_rows = queries[0].reshape(tok_rows, H, HD)
    gradient_by_head = attn_grad.reshape(tok_rows, H, HD)
    out_heads = attn_out[0].reshape(tok_rows, H, HD)
    dots_round = jnp.sum(
        gradient_by_head.astype(jnp.float32) * out_heads.astype(jnp.float32), axis=-1
    ).astype(jnp.bfloat16)
    own_rows = jnp.repeat(
        lax.dynamic_slice_in_dim(tile_table, ctx_index * own_count, own_count, 1).astype(
            jnp.float32
        ),
        TILE,
        axis=1,
    )
    norm_rows = log_norm[0].astype(jnp.float32)
    dots_rows = lax.optimization_barrier(dots_round).astype(jnp.float32)
    key_rows = lax.all_gather(key_states[0], "ctx", axis=0, tiled=True)
    value_rows = lax.all_gather(value_states[0], "ctx", axis=0, tiled=True)
    piece_rows = key_rows.shape[0]
    sub_rows = min(piece_rows, tok_rows)
    blocks_in = piece_rows // sub_rows
    key_block = key_rows.reshape(piece_rows, H, HD)
    value_block = value_rows.reshape(piece_rows, H, HD)
    allowed = jnp.einsum("htn,mn->htm", own_rows, tile_onehot(piece_rows, tile_count))
    probability_per_round, gradient_per_round = score_terms(
        query_head_rows, gradient_by_head, norm_rows, dots_rows, key_block, value_block, allowed
    )
    value_term = jnp.einsum(
        "bve,vbt->ebt", probability_per_round, gradient_by_head, preferred_element_type=jnp.float32
    )
    key_term = (
        jnp.einsum(
            "bve,vbt->ebt", gradient_per_round, query_head_rows, preferred_element_type=jnp.float32
        )
        * score_scale
    )
    query_term = (
        jnp.einsum(
            "hmbn,bnhd->bmhd",
            gradient_per_round.reshape(H, tok_rows, blocks_in, sub_rows),
            key_block.reshape(blocks_in, sub_rows, H, HD),
            preferred_element_type=jnp.float32,
        )
        * score_scale
    )
    part_slots = query_term.reshape(blocks_in, tok_rows, hid_width)
    key_total = key_term.reshape(piece_rows, hid_width)
    value_total = value_term.reshape(piece_rows, hid_width)
    part_slots, key_total, value_total = (part_slots, key_total, value_total)
    grad_query = jnp.sum(round_trip(part_slots), axis=0).astype(jnp.bfloat16)
    key_parts, value_parts = (
        lax.all_to_all(
            key_total.astype(jnp.bfloat16).reshape(ctx_count, tok_rows, hid_width),
            "ctx",
            split_axis=0,
            concat_axis=0,
            tiled=True,
        ),
        lax.all_to_all(
            value_total.astype(jnp.bfloat16).reshape(ctx_count, tok_rows, hid_width),
            "ctx",
            split_axis=0,
            concat_axis=0,
            tiled=True,
        ),
    )
    grad_key = jnp.sum(key_parts.astype(jnp.float32), axis=0).astype(jnp.bfloat16)
    grad_value = jnp.sum(value_parts.astype(jnp.float32), axis=0).astype(jnp.bfloat16)
    return (grad_query[None], grad_key[None], grad_value[None])


MESH = pl.DeviceIdType.MESH
CHUNKS = 2
UP, DOWN, ACROSS, SIBLING = range(4)


def dot(a, b, a_dim, b_dim):
    return lax.dot_general(
        a, b, (((a_dim,), (b_dim,)), ((), ())), preferred_element_type=jnp.float32
    )


def fused_kernel(
    q_ref, k_ref, v_ref, o_ref, ln_ref, og_ref, w_ref, mask_ref,
    gq_ref, gk_ref, gv_ref,
    wbuf, og_all, q_all, k_all, v_all, o_all, ln_all, p_all,
    part_own, part_in, grad, dots, dq_out, dq_in,
    w_send, w_recv, x_send, x_recv, local_sem,
):
    layers = wbuf.shape[0]
    chunk_rows = wbuf.shape[3] // CHUNKS
    tok = q_ref.shape[1]
    heads = ln_ref.shape[2]
    width = w_ref.shape[1]
    group_width = grad.shape[2]
    per_group = heads // layers
    hd = group_width // per_group
    tile = 2 * tok // mask_ref.shape[2]
    own_tiles = tok // tile
    scale = hd ** (-0.5)

    f = lax.axis_index("fsdp")
    x = lax.axis_index("ctx")
    core = lax.rem(f, 2)
    y = lax.rem(lax.div(f, 2), 2)
    z = lax.div(f, 4)
    other = 1 - x

    def place(zz, yy, cc):
        return ((zz * 2 + yy) * 2 + cc, x)

    partner = (f, other)
    targets = {
        UP: place(z + 1, y, core),
        DOWN: place(z - 1, y, core),
        ACROSS: place(z, 1 - y, core),
        SIBLING: place(z, y, 1 - core),
    }
    has_up = z < layers - 1
    has_down = z > 0

    own_block = pl.ds(pl.multiple_of(x * width, width), width)
    load_w, load_og, load_q, load_k, load_v, load_o = (
        pltpu.make_async_copy(source, target, local_sem.at[n])
        for n, (source, target) in enumerate(
            (
                (w_ref, wbuf.at[z, y, core]),
                (og_ref.at[0, :, own_block], og_all.at[pl.ds(0, tok)]),
                (q_ref.at[0], q_all.at[pl.ds(0, tok)]),
                (k_ref.at[0], k_all),
                (v_ref.at[0], v_all),
                (o_ref.at[0], o_all),
            )
        )
    )
    for load in (load_q, load_k, load_og, load_w, load_v, load_o):
        load.start()

    barrier = pltpu.get_barrier_semaphore()
    for device in (partner, targets[ACROSS], targets[SIBLING]):
        pl.semaphore_signal(barrier, inc=1, device_id=device, device_id_type=MESH)

    @pl.when(has_up)
    def _():
        pl.semaphore_signal(barrier, inc=1, device_id=targets[UP], device_id_type=MESH)

    @pl.when(has_down)
    def _():
        pl.semaphore_signal(barrier, inc=1, device_id=targets[DOWN], device_id_type=MESH)

    pl.semaphore_wait(barrier, 3 + has_up.astype(jnp.int32) + has_down.astype(jnp.int32))

    def weight_copy(zz, yy, cc, ch, way, own=False):
        rows = pl.ds(ch * chunk_rows, chunk_rows)
        slot = wbuf.at[zz, yy, cc, rows]
        source = w_ref.at[rows] if own else slot
        return pltpu.make_async_remote_copy(
            src_ref=source,
            dst_ref=slot,
            send_sem=w_send.at[zz, yy, cc, ch, way],
            recv_sem=w_recv.at[zz, yy, cc, ch],
            device_id=targets[way],
            device_id_type=MESH,
        )

    def x_copy(source, target, kind, k=0):
        return pltpu.make_async_remote_copy(
            src_ref=source,
            dst_ref=target,
            send_sem=x_send.at[kind, k],
            recv_sem=x_recv.at[kind, k],
            device_id=partner,
            device_id_type=MESH,
        )

    og_copy = x_copy(
        og_ref.at[0, :, pl.ds(pl.multiple_of(other * width, width), width)],
        og_all.at[pl.ds(tok, tok)],
        0,
    )
    q_copy = x_copy(q_ref.at[0], q_all.at[pl.ds(tok, tok)], 1)
    ln_copy = x_copy(ln_all.at[0], ln_all.at[1], 2)

    def part_copies(k):
        return (
            x_copy(part_own.at[k, pl.ds(tok, tok)], part_in.at[k, pl.ds(0, tok)], 3, k),
            x_copy(part_own.at[k, pl.ds(0, tok)], part_in.at[k, pl.ds(tok, tok)], 4, k),
        )

    def dots_copy(k):
        return x_copy(dots.at[k, 0], dots.at[k, 1], 5, k)

    def dq_copy(k):
        return x_copy(dq_out.at[k], dq_in.at[k], 6, k)

    def own_weight(action):
        for ch in range(CHUNKS):
            for way, there in ((UP, has_up), (DOWN, has_down), (ACROSS, None), (SIBLING, None)):
                def run(way=way, ch=ch):
                    action(weight_copy(z, y, core, ch, way, True))

                if there is None:
                    run()
                else:
                    pl.when(there)(run)

    own_weight(lambda copy: copy.start())
    og_copy.start()
    ln_all[0] = jnp.zeros(ln_all.shape[1:], ln_all.dtype)
    ln_all[0, :, pl.ds(0, heads)] = ln_ref[0]
    ln_copy.start()

    def handle_z(d):
        for ch in range(CHUNKS):

            @pl.when(z >= d)
            def _(ch=ch):
                weight_copy(z - d, y, core, ch, SIBLING).wait_recv()

                @pl.when(has_up)
                def _():
                    weight_copy(z - d, y, core, ch, UP).start()

                weight_copy(z - d, y, core, ch, ACROSS).start()
                weight_copy(z - d, y, core, ch, SIBLING).start()

            @pl.when(z + d < layers)
            def _(ch=ch):
                weight_copy(z + d, y, core, ch, SIBLING).wait_recv()

                @pl.when(has_down)
                def _():
                    weight_copy(z + d, y, core, ch, DOWN).start()

                weight_copy(z + d, y, core, ch, ACROSS).start()
                weight_copy(z + d, y, core, ch, SIBLING).start()

    def handle_y(d):
        for ch in range(CHUNKS):

            @pl.when(z >= d)
            def _(ch=ch):
                weight_copy(z - d, 1 - y, core, ch, SIBLING).wait_recv()
                weight_copy(z - d, 1 - y, core, ch, SIBLING).start()

            if d:

                @pl.when(z + d < layers)
                def _(ch=ch):
                    weight_copy(z + d, 1 - y, core, ch, SIBLING).wait_recv()
                    weight_copy(z + d, 1 - y, core, ch, SIBLING).start()

    def wait_siblings(g):
        for ch in range(CHUNKS):
            weight_copy(g, y, 1 - core, ch, SIBLING).wait_recv()
            weight_copy(g, 1 - y, 1 - core, ch, SIBLING).wait_recv()

    turn = 1 - 2 * lax.div(z, layers // 2)

    def layer(k):
        return lax.rem(z + turn * k + layers, layers)

    lane_tile = lax.div(lax.broadcasted_iota(jnp.int32, (1, tok), 1), tile)

    def probabilities(b, owner):
        norm = ln_all[b].astype(jnp.float32)
        for h in range(heads):
            cols = pl.ds(h * hd, hd)
            scores = dot(q_all[pl.ds(b * tok, tok), cols], k_all[:, cols], 1, 1) * scale
            prob = jnp.exp(scores - norm[:, h : h + 1])
            for i in range(own_tiles):
                allowed = jnp.zeros((1, tok), jnp.float32)
                for j in range(own_tiles):
                    flag = mask_ref[0, owner * own_tiles + i, x * own_tiles + j, h]
                    allowed = jnp.where(lane_tile == j, flag.astype(jnp.float32), allowed)
                p_all[h, pl.ds(b * tok + i * tile, tile), :] = (
                    prob[i * tile : (i + 1) * tile] * allowed
                )

    def project(k):
        g = layer(k)
        wait_siblings(g)
        w = wbuf[g].reshape(group_width, width)
        for b in (1, 0):
            part = dot(og_all[pl.ds(b * tok, tok)], w, 1, 1)
            part_own[k, pl.ds(b * tok, tok)] = part.astype(jnp.bfloat16)
            part_copies(k)[1 - b].start()

    lane = lax.broadcasted_iota(jnp.int32, (tok, dots.shape[3]), 1)

    def reduce(k):
        g = layer(k)
        for copy in part_copies(k):
            copy.wait_recv()
        total = part_own[k].astype(jnp.float32) + part_in[k].astype(jnp.float32)
        total = total.astype(jnp.bfloat16)
        grad[k] = total
        own = total[:tok].astype(jnp.float32)
        row = jnp.zeros(lane.shape, jnp.float32)
        for j in range(per_group):
            cols = pl.ds(pl.multiple_of((g * per_group + j) * hd, hd), hd)
            prod = own[:, j * hd : (j + 1) * hd] * o_all[:, cols].astype(jnp.float32)
            row = jnp.where(lane == j, jnp.sum(prod, axis=1, keepdims=True), row)
        dots[k, 0] = row.astype(jnp.bfloat16)
        dots_copy(k).start()

    def attend(k):
        g = layer(k)
        dots_copy(k).wait_recv()
        row = dots[k].reshape(2 * tok, dots.shape[3]).astype(jnp.float32)
        for j in range(per_group):
            h = g * per_group + j
            cols = pl.ds(pl.multiple_of(h * hd, hd), hd)
            prob = p_all[h]
            grad_rows = grad[k, :, pl.ds(j * hd, hd)]
            prob_grad = dot(grad_rows, v_all[:, cols], 1, 1)
            score_grad = (prob * (prob_grad - row[:, j : j + 1])).astype(jnp.bfloat16)
            part = dot(score_grad, k_all[:, cols], 1, 0) * scale
            part = part.astype(jnp.bfloat16)
            dq_out[k, :, pl.ds(j * hd, hd)] = part[tok:]
            gq_ref[0, :, cols] = part[:tok]
            gv_ref[0, :, cols] = dot(prob.astype(jnp.bfloat16), grad_rows, 0, 0).astype(
                jnp.bfloat16
            )
            gk_ref[0, :, cols] = (dot(score_grad, q_all[:, cols], 0, 0) * scale).astype(
                jnp.bfloat16
            )
        dq_copy(k).start()

    def finish(k):
        g = layer(k)
        cols = pl.ds(pl.multiple_of(g * group_width, group_width), group_width)
        dq_copy(k).wait_recv()
        gq_ref[0, :, cols] = (
            gq_ref[0, :, cols].astype(jnp.float32) + dq_in[k].astype(jnp.float32)
        ).astype(jnp.bfloat16)

    handle_z(1)
    handle_y(0)
    load_q.wait()
    load_k.wait()
    probabilities(0, x)
    og_copy.wait_recv()
    q_copy.start()
    load_og.wait()
    load_w.wait()
    for k in range(layers + 3):
        if k < layers:
            project(k)
            if k + 2 < layers:
                handle_z(k + 2)
            if k + 1 < layers:
                handle_y(k + 1)
        if k == 1:
            ln_copy.wait_recv()
            q_copy.wait_recv()
            probabilities(1, other)
            load_v.wait()
        if k == 0:
            load_o.wait()
        if 0 <= k - 1 < layers:
            reduce(k - 1)
        if 0 <= k - 2 < layers:
            attend(k - 2)
        if 0 <= k - 3 < layers:
            finish(k - 3)

    own_weight(lambda copy: copy.wait_send())
    for ch in range(CHUNKS):
        weight_copy(z, 1 - y, core, ch, SIBLING).wait_send()
    for d in range(1, layers):
        for ch in range(CHUNKS):

            @pl.when(z >= d)
            def _(ch=ch, d=d):
                @pl.when(has_up)
                def _():
                    weight_copy(z - d, y, core, ch, UP).wait_send()

                weight_copy(z - d, y, core, ch, ACROSS).wait_send()
                weight_copy(z - d, y, core, ch, SIBLING).wait_send()
                weight_copy(z - d, 1 - y, core, ch, SIBLING).wait_send()

            @pl.when(z + d < layers)
            def _(ch=ch, d=d):
                @pl.when(has_down)
                def _():
                    weight_copy(z + d, y, core, ch, DOWN).wait_send()

                weight_copy(z + d, y, core, ch, ACROSS).wait_send()
                weight_copy(z + d, y, core, ch, SIBLING).wait_send()
                weight_copy(z + d, 1 - y, core, ch, SIBLING).wait_send()

    og_copy.wait_send()
    q_copy.wait_send()
    ln_copy.wait_send()
    for k in range(layers):
        for copy in part_copies(k):
            copy.wait_send()
        dots_copy(k).wait_send()
        dq_copy(k).wait_send()


def fits_kernel(queries, key_states, value_states, attn_out, log_norm, out_grad, proj_weight, tile_mask):
    fsdp = lax.axis_size("fsdp")
    heads = log_norm.shape[2]
    tok = queries.shape[1]
    rows = proj_weight.shape[0]
    if lax.axis_size("ctx") != 2 or fsdp % 8 or queries.shape[0] != 1:
        return False
    layers = fsdp // 4
    head_size = queries.shape[2] // heads
    return (
        heads % layers == 0
        and rows % (16 * CHUNKS) == 0
        and head_size == 128
        and tok % 128 == 0
        and tok % (2 * tok // tile_mask.shape[3]) == 0
        and proj_weight.shape[1] % 128 == 0
    )


def fused(queries, key_states, value_states, attn_out, log_norm, out_grad, proj_weight, tile_mask):
    layers = lax.axis_size("fsdp") // 4
    tok, hid = queries.shape[1:]
    rows, width = proj_weight.shape
    heads = log_norm.shape[2]
    group = hid // layers
    bf16 = jnp.bfloat16
    whole = pl.BlockSpec(memory_space=pltpu.VMEM)
    far = pl.BlockSpec(memory_space=pl.ANY)
    mask = jnp.transpose(tile_mask, (0, 2, 3, 1))
    return tuple(pl.pallas_call(
        fused_kernel,
        out_shape=[jax.ShapeDtypeStruct(queries.shape, bf16)] * 3,
        in_specs=[far] * 4 + [whole] + [far] * 2 + [pl.BlockSpec(memory_space=pltpu.SMEM)],
        out_specs=[whole] * 3,
        scratch_shapes=[
            pltpu.VMEM((layers, 2, 2, rows, width), bf16),
            pltpu.VMEM((2 * tok, width), bf16),
            pltpu.VMEM((2 * tok, hid), bf16),
            pltpu.VMEM((tok, hid), bf16),
            pltpu.VMEM((tok, hid), bf16),
            pltpu.VMEM((tok, hid), bf16),
            pltpu.VMEM((2, tok, 128), bf16),
            pltpu.VMEM((heads, 2 * tok, tok), jnp.float32),
            pltpu.VMEM((layers, 2 * tok, group), bf16),
            pltpu.VMEM((layers, 2 * tok, group), bf16),
            pltpu.VMEM((layers, 2 * tok, group), bf16),
            pltpu.VMEM((layers, 2, tok, 128), bf16),
            pltpu.VMEM((layers, tok, group), bf16),
            pltpu.VMEM((layers, tok, group), bf16),
            pltpu.SemaphoreType.DMA((layers, 2, 2, CHUNKS, 4)),
            pltpu.SemaphoreType.DMA((layers, 2, 2, CHUNKS)),
            pltpu.SemaphoreType.DMA((7, layers)),
            pltpu.SemaphoreType.DMA((7, layers)),
            pltpu.SemaphoreType.DMA((6,)),
        ],
        compiler_params=pltpu.CompilerParams(
            collective_id=0, has_side_effects=True, vmem_limit_bytes=56 * 1024 * 1024
        ),
    )(queries, key_states, value_states, attn_out, log_norm, out_grad, proj_weight, mask))


def plan(*arrays):
    if fits_kernel(*arrays):
        return fused(*arrays)
    return local(*arrays)


def solution(mesh):
    placed = (
        P("fsdp", "ctx", None),
        P("fsdp", "ctx", None),
        P("fsdp", "ctx", None),
        P("fsdp", "ctx", None),
        P("fsdp", "ctx", None),
        P("fsdp", "ctx", None),
        P("fsdp", "ctx"),
        P("fsdp", None, None, None),
    )
    return jax.shard_map(
        plan,
        mesh=mesh,
        in_specs=placed,
        out_specs=(P("fsdp", "ctx", None), P("fsdp", "ctx", None), P("fsdp", "ctx", None)),
        check_vma=False,
    )
```

```python
import functools

import jax
import jax.numpy as jnp
from jax import lax
from jax.experimental import pallas as pl
from jax.experimental.pallas import tpu as pltpu
from jax.sharding import PartitionSpec as P

H = 12
HD = 128
TILE = 64


def round_trip(array):
    return lax.optimization_barrier(array.astype(jnp.bfloat16)).astype(jnp.float32)


def tile_onehot(row_count, tile_count):
    tile_ids = jnp.arange(row_count, dtype=jnp.int32) // TILE
    return (tile_ids[:, None] == jnp.arange(tile_count, dtype=jnp.int32)[None, :]).astype(
        jnp.float32
    )


def score_terms(
    query_head_rows, gradient_by_head, norm_rows, dots_rows, key_head_rows, value_head_rows, allowed
):
    score_scale = HD ** (-0.5)
    scores = (
        jnp.einsum(
            "vgl,ygl->gvy", query_head_rows, key_head_rows, preferred_element_type=jnp.float32
        )
        * score_scale
    )
    attn_prob = jnp.exp(scores - norm_rows.T[:, :, None]) * allowed
    prob_grad = jnp.einsum(
        "vgl,ygl->gvy", gradient_by_head, value_head_rows, preferred_element_type=jnp.float32
    )
    score_grad = attn_prob * (prob_grad - dots_rows.T[:, :, None])
    return (attn_prob.astype(jnp.bfloat16), score_grad.astype(jnp.bfloat16))


def local(queries, key_states, value_states, attn_out, log_norm, out_grad, proj_weight, tile_mask):
    ctx_count = lax.axis_size("ctx")
    ctx_index = lax.axis_index("ctx")
    tok_rows = queries.shape[1]
    hid_width = queries.shape[2]
    score_scale = HD ** (-0.5)
    tile_table = tile_mask[0]
    tile_count = tile_table.shape[1]
    own_count = tok_rows // TILE
    grad_slab = lax.all_to_all(out_grad[0], "ctx", split_axis=1, concat_axis=0, tiled=True)
    product = lax.dot_general(
        grad_slab,
        lax.all_gather(proj_weight, "fsdp", axis=0, tiled=True),
        (((1,), (1,)), ((), ())),
        preferred_element_type=jnp.float32,
    )
    partial_value = product.astype(jnp.bfloat16)
    arrived = lax.all_to_all(
        partial_value.reshape(ctx_count, tok_rows, hid_width),
        "ctx",
        split_axis=0,
        concat_axis=0,
        tiled=True,
    )
    attn_grad = jnp.sum(arrived.astype(jnp.float32), axis=0).astype(jnp.bfloat16)
    query_head_rows = queries[0].reshape(tok_rows, H, HD)
    gradient_by_head = attn_grad.reshape(tok_rows, H, HD)
    out_heads = attn_out[0].reshape(tok_rows, H, HD)
    dots_round = jnp.sum(
        gradient_by_head.astype(jnp.float32) * out_heads.astype(jnp.float32), axis=-1
    ).astype(jnp.bfloat16)
    own_rows = jnp.repeat(
        lax.dynamic_slice_in_dim(tile_table, ctx_index * own_count, own_count, 1).astype(
            jnp.float32
        ),
        TILE,
        axis=1,
    )
    norm_rows = log_norm[0].astype(jnp.float32)
    dots_rows = lax.optimization_barrier(dots_round).astype(jnp.float32)
    key_rows = lax.all_gather(key_states[0], "ctx", axis=0, tiled=True)
    value_rows = lax.all_gather(value_states[0], "ctx", axis=0, tiled=True)
    piece_rows = key_rows.shape[0]
    sub_rows = min(piece_rows, tok_rows)
    blocks_in = piece_rows // sub_rows
    key_block = key_rows.reshape(piece_rows, H, HD)
    value_block = value_rows.reshape(piece_rows, H, HD)
    allowed = jnp.einsum("htn,mn->htm", own_rows, tile_onehot(piece_rows, tile_count))
    probability_per_round, gradient_per_round = score_terms(
        query_head_rows, gradient_by_head, norm_rows, dots_rows, key_block, value_block, allowed
    )
    value_term = jnp.einsum(
        "bve,vbt->ebt", probability_per_round, gradient_by_head, preferred_element_type=jnp.float32
    )
    key_term = (
        jnp.einsum(
            "bve,vbt->ebt", gradient_per_round, query_head_rows, preferred_element_type=jnp.float32
        )
        * score_scale
    )
    query_term = (
        jnp.einsum(
            "hmbn,bnhd->bmhd",
            gradient_per_round.reshape(H, tok_rows, blocks_in, sub_rows),
            key_block.reshape(blocks_in, sub_rows, H, HD),
            preferred_element_type=jnp.float32,
        )
        * score_scale
    )
    part_slots = query_term.reshape(blocks_in, tok_rows, hid_width)
    key_total = key_term.reshape(piece_rows, hid_width)
    value_total = value_term.reshape(piece_rows, hid_width)
    part_slots, key_total, value_total = (part_slots, key_total, value_total)
    grad_query = jnp.sum(round_trip(part_slots), axis=0).astype(jnp.bfloat16)
    key_parts, value_parts = (
        lax.all_to_all(
            key_total.astype(jnp.bfloat16).reshape(ctx_count, tok_rows, hid_width),
            "ctx",
            split_axis=0,
            concat_axis=0,
            tiled=True,
        ),
        lax.all_to_all(
            value_total.astype(jnp.bfloat16).reshape(ctx_count, tok_rows, hid_width),
            "ctx",
            split_axis=0,
            concat_axis=0,
            tiled=True,
        ),
    )
    grad_key = jnp.sum(key_parts.astype(jnp.float32), axis=0).astype(jnp.bfloat16)
    grad_value = jnp.sum(value_parts.astype(jnp.float32), axis=0).astype(jnp.bfloat16)
    return (grad_query[None], grad_key[None], grad_value[None])


MESH = pl.DeviceIdType.MESH
CHUNKS = 1
UP, DOWN, ACROSS, SIBLING = range(4)


def dot(a, b, a_dim, b_dim):
    return lax.dot_general(
        a, b, (((a_dim,), (b_dim,)), ((), ())), preferred_element_type=jnp.float32
    )


def fused_kernel(
    q_ref, k_ref, v_ref, o_ref, ln_ref, og_ref, w_ref, mask_ref,
    gq_ref, gk_ref, gv_ref,
    wbuf, og_all, q_all, k_all, v_all, o_all, ln_all, p_all,
    part_own, part_in, grad, dots, dq_out, dq_in,
    w_send, w_recv, x_send, x_recv, local_sem,
):
    layers = wbuf.shape[0]
    chunk_rows = wbuf.shape[3] // CHUNKS
    tok = q_ref.shape[1]
    heads = ln_ref.shape[1]
    width = w_ref.shape[1]
    group_width = grad.shape[2]
    per_group = heads // layers
    hd = group_width // per_group
    tile = 2 * tok // mask_ref.shape[2]
    own_tiles = tok // tile
    scale = hd ** (-0.5)

    f = lax.axis_index("fsdp")
    x = lax.axis_index("ctx")
    core = lax.rem(f, 2)
    y = lax.rem(lax.div(f, 2), 2)
    z = lax.div(f, 4)
    other = 1 - x

    def place(zz, yy, cc):
        return ((zz * 2 + yy) * 2 + cc, x)

    partner = (f, other)
    targets = {
        UP: place(z + 1, y, core),
        DOWN: place(z - 1, y, core),
        ACROSS: place(z, 1 - y, core),
        SIBLING: place(z, y, 1 - core),
    }
    has_up = z < layers - 1
    has_down = z > 0

    own_block = pl.ds(pl.multiple_of(x * width, width), width)
    load_w, load_og, load_q, load_k, load_v, load_o = (
        pltpu.make_async_copy(source, target, local_sem.at[n])
        for n, (source, target) in enumerate(
            (
                (w_ref, wbuf.at[z, y, core]),
                (og_ref.at[0, :, own_block], og_all.at[pl.ds(0, tok)]),
                (q_ref.at[0], q_all.at[pl.ds(0, tok)]),
                (k_ref.at[0], k_all),
                (v_ref.at[0], v_all),
                (o_ref.at[0], o_all),
            )
        )
    )
    for load in (load_q, load_k, load_og, load_w, load_v, load_o):
        load.start()

    barrier = pltpu.get_barrier_semaphore()
    for device in (partner, targets[ACROSS], targets[SIBLING]):
        pl.semaphore_signal(barrier, inc=1, device_id=device, device_id_type=MESH)

    @pl.when(has_up)
    def _():
        pl.semaphore_signal(barrier, inc=1, device_id=targets[UP], device_id_type=MESH)

    @pl.when(has_down)
    def _():
        pl.semaphore_signal(barrier, inc=1, device_id=targets[DOWN], device_id_type=MESH)

    pl.semaphore_wait(barrier, 3 + has_up.astype(jnp.int32) + has_down.astype(jnp.int32))

    def weight_copy(zz, yy, cc, ch, way, own=False):
        rows = pl.ds(ch * chunk_rows, chunk_rows)
        slot = wbuf.at[zz, yy, cc, rows]
        source = w_ref.at[rows] if own else slot
        return pltpu.make_async_remote_copy(
            src_ref=source,
            dst_ref=slot,
            send_sem=w_send.at[zz, yy, cc, ch, way],
            recv_sem=w_recv.at[zz, yy, cc, ch],
            device_id=targets[way],
            device_id_type=MESH,
        )

    def x_copy(source, target, kind, k=0):
        return pltpu.make_async_remote_copy(
            src_ref=source,
            dst_ref=target,
            send_sem=x_send.at[kind, k],
            recv_sem=x_recv.at[kind, k],
            device_id=partner,
            device_id_type=MESH,
        )

    og_copy = x_copy(
        og_ref.at[0, :, pl.ds(pl.multiple_of(other * width, width), width)],
        og_all.at[pl.ds(tok, tok)],
        0,
    )
    q_copy = x_copy(q_ref.at[0], q_all.at[pl.ds(tok, tok)], 1)
    ln_copy = x_copy(ln_all.at[0], ln_all.at[1], 2)

    def part_copies(k):
        return (
            x_copy(part_own.at[k, pl.ds(tok, tok)], part_in.at[k, pl.ds(0, tok)], 3, k),
            x_copy(part_own.at[k, pl.ds(0, tok)], part_in.at[k, pl.ds(tok, tok)], 4, k),
        )

    def dots_copy(k):
        return x_copy(dots.at[k, 0], dots.at[k, 1], 5, k)

    def dq_copy(k):
        return x_copy(dq_out.at[k], dq_in.at[k], 6, k)

    def own_weight(action):
        for ch in range(CHUNKS):
            for way, there in ((UP, has_up), (DOWN, has_down), (ACROSS, None), (SIBLING, None)):
                def run(way=way, ch=ch):
                    action(weight_copy(z, y, core, ch, way, True))

                if there is None:
                    run()
                else:
                    pl.when(there)(run)

    own_weight(lambda copy: copy.start())
    og_copy.start()
    ln_all[0] = jnp.zeros(ln_all.shape[1:], ln_all.dtype)
    ln_all[0, pl.ds(0, heads), :] = ln_ref[0]
    ln_copy.start()

    def handle_z(d):
        for ch in range(CHUNKS):

            @pl.when(z >= d)
            def _(ch=ch):
                weight_copy(z - d, y, core, ch, SIBLING).wait_recv()

                @pl.when(has_up)
                def _():
                    weight_copy(z - d, y, core, ch, UP).start()

                weight_copy(z - d, y, core, ch, ACROSS).start()
                weight_copy(z - d, y, core, ch, SIBLING).start()

            @pl.when(z + d < layers)
            def _(ch=ch):
                weight_copy(z + d, y, core, ch, SIBLING).wait_recv()

                @pl.when(has_down)
                def _():
                    weight_copy(z + d, y, core, ch, DOWN).start()

                weight_copy(z + d, y, core, ch, ACROSS).start()
                weight_copy(z + d, y, core, ch, SIBLING).start()

    def handle_y(d):
        for ch in range(CHUNKS):

            @pl.when(z >= d)
            def _(ch=ch):
                weight_copy(z - d, 1 - y, core, ch, SIBLING).wait_recv()
                weight_copy(z - d, 1 - y, core, ch, SIBLING).start()

            if d:

                @pl.when(z + d < layers)
                def _(ch=ch):
                    weight_copy(z + d, 1 - y, core, ch, SIBLING).wait_recv()
                    weight_copy(z + d, 1 - y, core, ch, SIBLING).start()

    def wait_siblings(g):
        for ch in range(CHUNKS):
            weight_copy(g, y, 1 - core, ch, SIBLING).wait_recv()
            weight_copy(g, 1 - y, 1 - core, ch, SIBLING).wait_recv()

    turn = 1 - 2 * lax.div(z, layers // 2)

    def layer(k):
        return lax.rem(z + turn * k + layers, layers)

    def spread(rows, h):
        pick = lax.broadcasted_iota(jnp.int32, (rows.shape[0], hd), 0) == h
        return dot(rows, jnp.where(pick, 1.0, 0.0).astype(jnp.bfloat16), 0, 0)

    lane_tile = lax.div(lax.broadcasted_iota(jnp.int32, (1, tok), 1), tile)

    def probabilities(b, owner):
        norm = ln_all[b]
        for h in range(heads):
            cols = pl.ds(h * hd, hd)
            scores = dot(q_all[pl.ds(b * tok, tok), cols], k_all[:, cols], 1, 1) * scale
            prob = jnp.exp(scores - spread(norm, h))
            for i in range(own_tiles):
                allowed = jnp.zeros((1, tok), jnp.float32)
                for j in range(own_tiles):
                    flag = mask_ref[0, owner * own_tiles + i, x * own_tiles + j, h]
                    allowed = jnp.where(lane_tile == j, flag.astype(jnp.float32), allowed)
                p_all[h, pl.ds(b * tok + i * tile, tile), :] = (
                    prob[i * tile : (i + 1) * tile] * allowed
                )

    def project(k):
        g = layer(k)
        wait_siblings(g)
        w = wbuf[g].reshape(group_width, width)
        for b in (1, 0):
            part = dot(og_all[pl.ds(b * tok, tok)], w, 1, 1)
            part_own[k, pl.ds(b * tok, tok)] = part.astype(jnp.bfloat16)
            part_copies(k)[1 - b].start()

    lane = lax.broadcasted_iota(jnp.int32, (tok, hd), 1)

    def reduce(k):
        g = layer(k)
        for copy in part_copies(k):
            copy.wait_recv()
        total = part_own[k].astype(jnp.float32) + part_in[k].astype(jnp.float32)
        total = total.astype(jnp.bfloat16)
        grad[k] = total
        own = total[:tok].astype(jnp.float32)
        row = jnp.zeros(lane.shape, jnp.float32)
        for j in range(per_group):
            cols = pl.ds(pl.multiple_of((g * per_group + j) * hd, hd), hd)
            prod = own[:, j * hd : (j + 1) * hd] * o_all[:, cols].astype(jnp.float32)
            row = jnp.where(lane == j, jnp.sum(prod, axis=1, keepdims=True), row)
        dots[k, 0] = jnp.transpose(row)[: dots.shape[2]].astype(jnp.bfloat16)
        dots_copy(k).start()

    def attend(k):
        g = layer(k)
        dots_copy(k).wait_recv()
        for j in range(per_group):
            h = g * per_group + j
            cols = pl.ds(pl.multiple_of(h * hd, hd), hd)
            prob = p_all[h]
            grad_rows = grad[k, :, pl.ds(j * hd, hd)]
            prob_grad = dot(grad_rows, v_all[:, cols], 1, 1)
            row = jnp.concatenate([spread(dots[k, 0], j), spread(dots[k, 1], j)], axis=0)
            score_grad = (prob * (prob_grad - row)).astype(jnp.bfloat16)
            part = dot(score_grad, k_all[:, cols], 1, 0) * scale
            part = part.astype(jnp.bfloat16)
            dq_out[k, :, pl.ds(j * hd, hd)] = part[tok:]
            gq_ref[0, :, cols] = part[:tok]
            gv_ref[0, :, cols] = dot(prob.astype(jnp.bfloat16), grad_rows, 0, 0).astype(
                jnp.bfloat16
            )
            gk_ref[0, :, cols] = (dot(score_grad, q_all[:, cols], 0, 0) * scale).astype(
                jnp.bfloat16
            )
        dq_copy(k).start()

    def finish(k):
        g = layer(k)
        cols = pl.ds(pl.multiple_of(g * group_width, group_width), group_width)
        dq_copy(k).wait_recv()
        gq_ref[0, :, cols] = (
            gq_ref[0, :, cols].astype(jnp.float32) + dq_in[k].astype(jnp.float32)
        ).astype(jnp.bfloat16)

    handle_z(1)
    handle_y(0)
    load_q.wait()
    load_k.wait()
    probabilities(0, x)
    og_copy.wait_recv()
    q_copy.start()
    load_og.wait()
    load_w.wait()
    for k in range(layers + 3):
        if k < layers:
            project(k)
            if k + 2 < layers:
                handle_z(k + 2)
            if k + 1 < layers:
                handle_y(k + 1)
        if k == 2:
            ln_copy.wait_recv()
            q_copy.wait_recv()
            probabilities(1, other)
            load_v.wait()
        if k == 0:
            load_o.wait()
        if 0 <= k - 1 < layers:
            reduce(k - 1)
        if 0 <= k - 2 < layers:
            attend(k - 2)
        if 0 <= k - 3 < layers:
            finish(k - 3)

    own_weight(lambda copy: copy.wait_send())
    for ch in range(CHUNKS):
        weight_copy(z, 1 - y, core, ch, SIBLING).wait_send()
    for d in range(1, layers):
        for ch in range(CHUNKS):

            @pl.when(z >= d)
            def _(ch=ch, d=d):
                @pl.when(has_up)
                def _():
                    weight_copy(z - d, y, core, ch, UP).wait_send()

                weight_copy(z - d, y, core, ch, ACROSS).wait_send()
                weight_copy(z - d, y, core, ch, SIBLING).wait_send()
                weight_copy(z - d, 1 - y, core, ch, SIBLING).wait_send()

            @pl.when(z + d < layers)
            def _(ch=ch, d=d):
                @pl.when(has_down)
                def _():
                    weight_copy(z + d, y, core, ch, DOWN).wait_send()

                weight_copy(z + d, y, core, ch, ACROSS).wait_send()
                weight_copy(z + d, y, core, ch, SIBLING).wait_send()
                weight_copy(z + d, 1 - y, core, ch, SIBLING).wait_send()

    og_copy.wait_send()
    q_copy.wait_send()
    ln_copy.wait_send()
    for k in range(layers):
        for copy in part_copies(k):
            copy.wait_send()
        dots_copy(k).wait_send()
        dq_copy(k).wait_send()


def fits_kernel(queries, key_states, value_states, attn_out, log_norm, out_grad, proj_weight, tile_mask):
    fsdp = lax.axis_size("fsdp")
    heads = log_norm.shape[2]
    tok = queries.shape[1]
    rows = proj_weight.shape[0]
    if lax.axis_size("ctx") != 2 or fsdp % 8 or fsdp < 12 or queries.shape[0] != 1:
        return False
    layers = fsdp // 4
    head_size = queries.shape[2] // heads
    return (
        heads % layers == 0
        and heads <= 16
        and tok == head_size
        and rows % (16 * CHUNKS) == 0
        and head_size == 128
        and tok % 128 == 0
        and tok % (2 * tok // tile_mask.shape[3]) == 0
        and proj_weight.shape[1] % 128 == 0
    )


def fused(queries, key_states, value_states, attn_out, log_norm, out_grad, proj_weight, tile_mask):
    layers = lax.axis_size("fsdp") // 4
    tok, hid = queries.shape[1:]
    rows, width = proj_weight.shape
    heads = log_norm.shape[2]
    norm = jnp.transpose(log_norm, (0, 2, 1))
    group = hid // layers
    bf16 = jnp.bfloat16
    whole = pl.BlockSpec(memory_space=pltpu.VMEM)
    far = pl.BlockSpec(memory_space=pl.ANY)
    mask = jnp.transpose(tile_mask, (0, 2, 3, 1))
    return tuple(pl.pallas_call(
        fused_kernel,
        out_shape=[jax.ShapeDtypeStruct(queries.shape, bf16)] * 3,
        in_specs=[far] * 4 + [whole] + [far] * 2 + [pl.BlockSpec(memory_space=pltpu.SMEM)],
        out_specs=[whole] * 3,
        scratch_shapes=[
            pltpu.VMEM((layers, 2, 2, rows, width), bf16),
            pltpu.VMEM((2 * tok, width), bf16),
            pltpu.VMEM((2 * tok, hid), bf16),
            pltpu.VMEM((tok, hid), bf16),
            pltpu.VMEM((tok, hid), bf16),
            pltpu.VMEM((tok, hid), bf16),
            pltpu.VMEM((2, 16, tok), bf16),
            pltpu.VMEM((heads, 2 * tok, tok), jnp.float32),
            pltpu.VMEM((layers, 2 * tok, group), bf16),
            pltpu.VMEM((layers, 2 * tok, group), bf16),
            pltpu.VMEM((layers, 2 * tok, group), bf16),
            pltpu.VMEM((layers, 2, 16, tok), bf16),
            pltpu.VMEM((layers, tok, group), bf16),
            pltpu.VMEM((layers, tok, group), bf16),
            pltpu.SemaphoreType.DMA((layers, 2, 2, CHUNKS, 4)),
            pltpu.SemaphoreType.DMA((layers, 2, 2, CHUNKS)),
            pltpu.SemaphoreType.DMA((7, layers)),
            pltpu.SemaphoreType.DMA((7, layers)),
            pltpu.SemaphoreType.DMA((6,)),
        ],
        compiler_params=pltpu.CompilerParams(
            collective_id=0, has_side_effects=True, vmem_limit_bytes=56 * 1024 * 1024
        ),
    )(queries, key_states, value_states, attn_out, norm, out_grad, proj_weight, mask))


def plan(*arrays):
    if fits_kernel(*arrays):
        return fused(*arrays)
    return local(*arrays)


def solution(mesh):
    placed = (
        P("fsdp", "ctx", None),
        P("fsdp", "ctx", None),
        P("fsdp", "ctx", None),
        P("fsdp", "ctx", None),
        P("fsdp", "ctx", None),
        P("fsdp", "ctx", None),
        P("fsdp", "ctx"),
        P("fsdp", None, None, None),
    )
    return jax.shard_map(
        plan,
        mesh=mesh,
        in_specs=placed,
        out_specs=(P("fsdp", "ctx", None), P("fsdp", "ctx", None), P("fsdp", "ctx", None)),
        check_vma=False,
    )
```
